256 devices in a mesh: blk: 64 (over y, x_hi, z), dp: 4 (over x_lo, core).
Axes of the slice: x: 4 (x_hi: 2, x_lo: 2; x = x_hi * 2 + x_lo), y: 4, z: 8, core: 2. Of those that a mesh axis runs over, the one named last changes fastest.
Arguments:
- documents: bfloat16 [393216, 1024], P(('blk', 'dp')), may hold values from -30 to 30
- centroids: bfloat16 [1024, 1024], P('blk'), may hold values from -6 to 6
Outputs:
- new_centroids: float32 [1024, 1024], P('blk')
- normalizer: float32 [393216], P(('blk', 'dp'))
The draws below stay inside these ranges and needn't reach their ends.
All inputs are finite; a program needn't handle non-finite values.
Results may differ from the reference program's by a relative error of at most 0.008.
Values may be sent and summed in bfloat16 or wider, within the bound.
No kernel may reach another device: no remote copies, remote signals or barrier semaphores. Data moves between devices by JAX's collectives and lax.ppermute only.
A program may use at most 64 MiB of HBM per device.

```python
import math
import jax
import jax.numpy as jnp
from jax import lax

D = 1024
DOC_DEV = 1536
K = 1024
NDOC = 393216


def pair_centroids(key):
    base = jax.random.normal(jax.random.fold_in(key, 11), (K, D), jnp.float32)
    return jnp.clip(base, -6.0, 6.0)


def draw_centroids(key, part):
    return pair_centroids(key).astype(jnp.bfloat16)


def draw_documents(key, part):
    key = jax.random.fold_in(key, 2)
    drawn = jnp.clip(jax.random.normal(key, (NDOC, D), jnp.float32), -6.0, 6.0)
    return drawn.astype(jnp.bfloat16)


def setup_inputs(seed: int = 0) -> dict:
    streams_of = jax.random.split(jax.random.key(seed), 3)
    return {
        "documents": draw_documents(jax.random.fold_in(streams_of[2], 71), 0),
        "centroids": draw_centroids(jax.random.fold_in(streams_of[2], 71), 0),
    }


def reference(documents, centroids):
    beta = 3.0 / math.sqrt(D)
    widened = centroids.astype(jnp.float32)
    norms = lax.optimization_barrier(jnp.sum(widened * widened, axis=1))
    blocks = documents.reshape(-1, DOC_DEV, D)

    def step(carry, block):
        sums, counts = carry
        logits = beta * jnp.dot(block, centroids.T, preferred_element_type=jnp.float32) - 0.5 * beta * norms[None, :]
        top = lax.optimization_barrier(jnp.max(logits, axis=1, keepdims=True))
        normal_row = top[:, 0] + jnp.log(lax.optimization_barrier(jnp.sum(jnp.exp(logits - top), axis=1)))
        weights = jnp.exp(logits - normal_row[:, None])
        counts = counts + lax.optimization_barrier(jnp.sum(weights, axis=0))
        sums = sums + jnp.dot(weights.astype(jnp.bfloat16).T, block, preferred_element_type=jnp.float32)
        return ((sums, counts), normal_row)
    start = (jnp.zeros((K, D), jnp.float32), jnp.zeros((K,), jnp.float32))
    (sums, counts), normalizer = lax.scan(step, start, blocks)
    new_centroids = (sums + widened) / (counts[:, None] + 1.0)
    return (new_centroids, normalizer.reshape(-1))
```

```python
import math

import jax
import jax.numpy as jnp
from jax import lax
from jax.sharding import Mesh, PartitionSpec as P

AXES = ("y", "xh", "z", "xl", "core")
SWAP = [(0, 1), (1, 0)]
OFFSETS = ((0, 1, -1, 2), (-2, 3, -3, 4))


def toward(j, sign):
    pairs = []
    for z in range(8):
        for core in range(2):
            far = ((z + OFFSETS[core][j]) % 8) * 2 + core
            near = z * 2 + core
            pairs.append((far, near) if sign > 0 else (near, far))
    return pairs


def scores(piece, norms, documents, beta):
    product = lax.dot_general(
        piece, documents, (((1,), (1,)), ((), ())), preferred_element_type=jnp.float32
    )
    return beta * product - 0.5 * beta * norms


def body(documents, centroids):
    beta = 3.0 / math.sqrt(documents.shape[1])
    width = documents.shape[1]
    others = lax.ppermute(documents, "core", SWAP)

    near = jnp.stack([lax.ppermute(centroids, ("z", "core"), toward(j, 1)) for j in range(4)])
    near = near.reshape(4, 2, 8, width).swapaxes(0, 1).reshape(1, 64, width)
    held = lax.all_to_all(
        jnp.broadcast_to(near, (8, 64, width)), ("y", "xh"), 0, 0, tiled=True
    ).reshape(512, width)

    widened = held.astype(jnp.float32)
    norms = jnp.sum(widened * widened, axis=1, keepdims=True)
    logits = (scores(held, norms, documents, beta), scores(held, norms, others, beta))
    tops = [jnp.max(part, axis=0) for part in logits]
    totals = [jnp.sum(jnp.exp(part - top[None, :]), axis=0) for part, top in zip(logits, tops)]
    mine = jnp.stack(tops + totals)
    theirs = lax.ppermute(mine, "core", SWAP)
    weights, normalizers = [], []
    for i in range(2):
        top = jnp.maximum(mine[i], theirs[1 - i])
        total = mine[2 + i] * jnp.exp(mine[i] - top) + theirs[3 - i] * jnp.exp(theirs[1 - i] - top)
        normalizers.append(top + jnp.log(total))
        weights.append(jnp.exp(logits[i] - normalizers[i][None, :]))
    counts = jnp.sum(weights[0], axis=1) + jnp.sum(weights[1], axis=1)
    sums = jnp.dot(weights[0].astype(jnp.bfloat16), documents, preferred_element_type=jnp.float32)
    sums += jnp.dot(weights[1].astype(jnp.bfloat16), others, preferred_element_type=jnp.float32)

    high = counts.astype(jnp.bfloat16)
    low = (counts - high.astype(jnp.float32)).astype(jnp.bfloat16)
    tail = jnp.pad(jnp.stack([high, low], axis=1), ((0, 0), (0, 126)))
    packed = jnp.concatenate([sums.astype(jnp.bfloat16), tail], axis=1).reshape(16, 32, -1)
    packed = lax.all_to_all(packed, ("y", "xh", "xl"), 0, 0, tiled=True)
    part = jnp.sum(packed.astype(jnp.float32), axis=0).reshape(4, 8, -1)
    part = sum(lax.ppermute(part[j], ("z", "core"), toward(j, -1)) for j in range(4))
    part = part + lax.ppermute(part, "core", SWAP)
    side = lax.axis_index("xl")
    own = lax.dynamic_slice_in_dim(centroids, side * 8, 8, 0).astype(jnp.float32)
    new = (part[:, :width] + own) / (part[:, width : width + 1] + part[:, width + 1 : width + 2] + 1.0)
    other = lax.ppermute(new, "xl", SWAP)
    first = side == 0
    new_centroids = jnp.concatenate([jnp.where(first, new, other), jnp.where(first, other, new)])
    return (new_centroids, normalizers[0])


def solution(mesh):
    fine = Mesh(mesh.devices.reshape(4, 2, 8, 2, 2), AXES)
    in_specs = (P(AXES, None), P(("y", "xh", "z"), None))
    out_specs = (P(("y", "xh", "z"), None), P(AXES))
    return jax.shard_map(body, mesh=fine, in_specs=in_specs, out_specs=out_specs, check_vma=False)
```

```python
import functools
import math

import jax
import jax.numpy as jnp
from jax import lax
from jax.experimental import pallas as pl
from jax.experimental.pallas import tpu as pltpu
from jax.sharding import Mesh, PartitionSpec as P

AXES = ("y", "xh", "z", "xl", "core")
SIZES = (4, 2, 8, 2, 2)
SWAP = [(0, 1), (1, 0)]
OFFSETS = ((0, 1, -1, 2), (-2, 3, -3, 4))
PEERS = 16
TILE = 512
MIB = 2**20


def toward(j, sign):
    pairs = []
    for z in range(8):
        for core in range(2):
            far = ((z + OFFSETS[core][j]) % 8) * 2 + core
            near = z * 2 + core
            pairs.append((far, near) if sign > 0 else (near, far))
    return pairs


def logits_kernel(beta, held, docs, others, logits, stats):
    count = docs.shape[0]
    block = held[...]
    wide = block.astype(jnp.float32)
    shift = (0.5 * beta) * jnp.sum(wide * wide, axis=1, keepdims=True)
    for side, source in enumerate((docs, others)):
        for start in range(0, count, TILE):
            part = lax.dot_general(
                block,
                source[start : start + TILE, :],
                (((1,), (1,)), ((), ())),
                preferred_element_type=jnp.float32,
            )
            part = beta * part - shift
            logits[:, side * count + start : side * count + start + TILE] = part
            top = jnp.max(part, axis=0, keepdims=True)
            stats[side : side + 1, start : start + TILE] = top
            stats[2 + side : 3 + side, start : start + TILE] = jnp.sum(
                jnp.exp(part - top), axis=0, keepdims=True
            )


def sums_kernel(logits, mine, theirs, docs, others, normalizer, packed, low):
    count = docs.shape[0]
    rows = logits.shape[0]
    per = rows // PEERS
    counts = jnp.zeros((rows, 128), jnp.float32)
    for side in range(2):
        a, b = mine[side : side + 1, :], theirs[1 - side : 2 - side, :]
        top = jnp.maximum(a, b)
        total = mine[2 + side : 3 + side, :] * jnp.exp(a - top)
        total += theirs[3 - side : 4 - side, :] * jnp.exp(b - top)
        norm = top + jnp.log(total)
        if side == 0:
            normalizer[...] = norm
        for start in range(0, count, TILE):
            at = side * count + start
            weights = jnp.exp(logits[:, at : at + TILE] - norm[:, start : start + TILE])
            for k in range(0, TILE, 128):
                counts += weights[:, k : k + 128]
            low[:, at : at + TILE] = weights.astype(jnp.bfloat16)
    flat = jnp.sum(counts.T, axis=0, keepdims=True)
    high = flat.astype(jnp.bfloat16)
    rest = (flat - high.astype(jnp.float32)).astype(jnp.bfloat16)
    slab = [part[:, k : k + 128] for part in (high, rest) for k in range(0, rows, 128)]
    slab = jnp.concatenate(slab + [jnp.zeros((16 - len(slab), 128), jnp.bfloat16)], axis=0)
    for peer in range(PEERS):
        packed[peer, per * 8 : per * 8 + 16, :] = slab
    for start in range(0, docs.shape[1], 256):
        columns = slice(start, start + 256)
        sums = jnp.dot(low[:, :count], docs[:, columns], preferred_element_type=jnp.float32)
        sums += jnp.dot(low[:, count:], others[:, columns], preferred_element_type=jnp.float32)
        sums = sums.astype(jnp.bfloat16)
        for half in range(2):
            tile = start // 128 + half
            packed[:, tile * per : (tile + 1) * per, :] = sums[:, half * 128 : half * 128 + 128].reshape(
                PEERS, per, 128
            )


def split_kernel(place, packed, *outs):
    per = 32
    total = jnp.sum(packed[...].astype(jnp.float32), axis=0)
    counts = total[per * 8 : per * 8 + 4, :] + total[per * 8 + 4 : per * 8 + 8, :]
    row = place[0] // 4
    counts = jnp.sum(
        jnp.where(lax.broadcasted_iota(jnp.int32, (4, 128), 0) == row, counts, 0.0), axis=0, keepdims=True
    )
    lane = lax.broadcasted_iota(jnp.int32, (per, 128), 1)
    wanted = lax.broadcasted_iota(jnp.int32, (per, 128), 0) + (place[0] - row * 4) * per
    counts = jnp.sum(jnp.where(lane == wanted, counts, 0.0), axis=1, keepdims=True)
    for j, out in enumerate(outs):
        for tile in range(8):
            out[tile] = total[tile * per + j * 8 : tile * per + j * 8 + 8, :]
        out[8] = jnp.broadcast_to(counts[j * 8 : j * 8 + 8, :], (8, 128))


def final_kernel(side, mine, core, across, diagonal, centroids, out):
    same = mine[...] + core[...]
    far = across[...] + diagonal[...]
    first = side[0] == 0
    for half, part in enumerate((jnp.where(first, same, far), jnp.where(first, far, same))):
        scale = part[8] + 1.0
        for tile in range(8):
            lanes = slice(tile * 128, tile * 128 + 128)
            own = centroids[half * 8 : half * 8 + 8, lanes].astype(jnp.float32)
            out[half * 8 : half * 8 + 8, lanes] = (part[tile] + own) / scale


def call(kernel, outs, vmem, operands, scalars=0, scratch=(), flops=0):
    whole = pl.BlockSpec(memory_space=pltpu.VMEM)
    in_specs = [pl.BlockSpec(memory_space=pltpu.SMEM)] * scalars + [whole] * (len(operands) - scalars)
    return pl.pallas_call(
        kernel,
        out_shape=[jax.ShapeDtypeStruct(shape, dtype) for shape, dtype in outs],
        in_specs=in_specs,
        out_specs=[whole] * len(outs),
        scratch_shapes=scratch,
        compiler_params=pltpu.CompilerParams(vmem_limit_bytes=vmem * MIB),
        cost_estimate=pl.CostEstimate(flops=flops, bytes_accessed=MIB, transcendentals=0),
    )(*operands)


def body(documents, centroids):
    count, width = documents.shape
    beta = 3.0 / math.sqrt(width)
    others = lax.ppermute(documents, "core", SWAP)

    near = jnp.stack([lax.ppermute(centroids, ("z", "core"), toward(j, 1)) for j in range(4)])
    near = near.reshape(4, 2, 8, width).swapaxes(0, 1).reshape(1, 64, width)
    held = lax.all_to_all(
        jnp.broadcast_to(near, (8, 64, width)), ("y", "xh"), 0, 0, tiled=True
    ).reshape(512, width)

    flops = 2 * 512 * 2 * count * width
    logits, mine = call(
        functools.partial(logits_kernel, beta),
        [((512, 2 * count), jnp.float32), ((4, count), jnp.float32)],
        20,
        (held, documents, others),
        flops=flops,
    )
    theirs = lax.ppermute(mine, "core", SWAP)
    normalizer, packed = call(
        sums_kernel,
        [((1, count), jnp.float32), ((PEERS, 272, 128), jnp.bfloat16)],
        24,
        (logits, mine, theirs, documents, others),
        scratch=[pltpu.VMEM((512, 2 * count), jnp.bfloat16)],
        flops=flops,
    )

    packed = lax.all_to_all(packed, ("y", "xh", "xl"), 0, 0, tiled=True)
    side = lax.axis_index("xl")
    place = (lax.axis_index("y") * 2 + lax.axis_index("xh")) * 2 + side
    parts = call(
        split_kernel, [((9, 8, 128), jnp.float32)] * 4, 8, (place.reshape(1), packed), scalars=1
    )
    part = sum(lax.ppermute(parts[j], ("z", "core"), toward(j, -1)) for j in range(4))
    diagonal, across, core = (
        lax.ppermute(part, ("xl", "core"), [(i, i ^ bits) for i in range(4)]) for bits in (3, 2, 1)
    )
    (new_centroids,) = call(
        final_kernel,
        [((16, width), jnp.float32)],
        4,
        (side.reshape(1), part, core, across, diagonal, centroids),
        scalars=1,
    )
    return (new_centroids, normalizer.reshape(count))


def solution(mesh):
    fine = Mesh(mesh.devices.reshape(SIZES), AXES)
    in_specs = (P(AXES, None), P(("y", "xh", "z"), None))
    out_specs = (P(("y", "xh", "z"), None), P(AXES))
    return jax.shard_map(body, mesh=fine, in_specs=in_specs, out_specs=out_specs, check_vma=False)
```

```python
import functools
import math

import jax
import jax.numpy as jnp
from jax import lax
from jax.experimental import pallas as pl
from jax.experimental.pallas import tpu as pltpu
from jax.sharding import Mesh, PartitionSpec as P

AXES = ("y", "xh", "zh", "zl", "xl", "core")
SIZES = (4, 2, 4, 2, 2, 2)
SWAP = [(0, 1), (1, 0)]
OFFSETS = ((0, 1), (-1, 2))
PEERS = 16
TILE = 512
MIB = 2**20


def toward(j, sign):
    pairs = []
    for zh in range(4):
        for core in range(2):
            far = ((zh + OFFSETS[core][j]) % 4) * 2 + core
            near = zh * 2 + core
            pairs.append((far, near) if sign > 0 else (near, far))
    return pairs


def logits_kernel(beta, held, docs, others, logits, stats):
    count = docs.shape[0]
    block = held[...]
    wide = block.astype(jnp.float32)
    shift = (0.5 * beta) * jnp.sum(wide * wide, axis=1, keepdims=True)
    for side, source in enumerate((docs, others)):
        for start in range(0, count, TILE):
            part = lax.dot_general(
                block,
                source[start : start + TILE, :],
                (((1,), (1,)), ((), ())),
                preferred_element_type=jnp.float32,
            )
            part = beta * part - shift
            logits[:, side * count + start : side * count + start + TILE] = part
            top = jnp.max(part, axis=0, keepdims=True)
            stats[side : side + 1, start : start + TILE] = top
            stats[2 + side : 3 + side, start : start + TILE] = jnp.sum(
                jnp.exp(part - top), axis=0, keepdims=True
            )


def sums_kernel(logits, mine, theirs, docs, others, normalizer, packed, low):
    count = docs.shape[0]
    rows = logits.shape[0]
    per = rows // PEERS
    counts = jnp.zeros((rows, 128), jnp.float32)
    for side in range(2):
        a, b = mine[side : side + 1, :], theirs[1 - side : 2 - side, :]
        top = jnp.maximum(a, b)
        total = mine[2 + side : 3 + side, :] * jnp.exp(a - top)
        total += theirs[3 - side : 4 - side, :] * jnp.exp(b - top)
        norm = top + jnp.log(total)
        if side == 0:
            normalizer[...] = norm
        for start in range(0, count, TILE):
            at = side * count + start
            weights = jnp.exp(logits[:, at : at + TILE] - norm[:, start : start + TILE])
            for k in range(0, TILE, 128):
                counts += weights[:, k : k + 128]
            low[:, at : at + TILE] = weights.astype(jnp.bfloat16)
    flat = jnp.sum(counts.T, axis=0, keepdims=True)
    high = flat.astype(jnp.bfloat16)
    rest = (flat - high.astype(jnp.float32)).astype(jnp.bfloat16)
    slab = [part[:, k : k + 128] for part in (high, rest) for k in range(0, rows, 128)]
    slab = jnp.concatenate(slab + [jnp.zeros((16 - len(slab), 128), jnp.bfloat16)], axis=0)
    for peer in range(PEERS):
        packed[peer, per * 8 : per * 8 + 16, :] = slab
    for start in range(0, docs.shape[1], 256):
        columns = slice(start, start + 256)
        sums = jnp.dot(low[:, :count], docs[:, columns], preferred_element_type=jnp.float32)
        sums += jnp.dot(low[:, count:], others[:, columns], preferred_element_type=jnp.float32)
        sums = sums.astype(jnp.bfloat16)
        for half in range(2):
            tile = start // 128 + half
            packed[:, tile * per : (tile + 1) * per, :] = sums[:, half * 128 : half * 128 + 128].reshape(
                PEERS, per, 128
            )


def split_kernel(place, packed, *outs):
    per = 32
    total = jnp.sum(packed[...].astype(jnp.float32), axis=0)
    counts = total[per * 8 : per * 8 + 4, :] + total[per * 8 + 4 : per * 8 + 8, :]
    row = place[0] // 4
    counts = jnp.sum(
        jnp.where(lax.broadcasted_iota(jnp.int32, (4, 128), 0) == row, counts, 0.0), axis=0, keepdims=True
    )
    lane = lax.broadcasted_iota(jnp.int32, (per, 128), 1)
    wanted = lax.broadcasted_iota(jnp.int32, (per, 128), 0) + (place[0] - row * 4) * per
    counts = jnp.sum(jnp.where(lane == wanted, counts, 0.0), axis=1, keepdims=True)
    for j, out in enumerate(outs):
        for tile in range(8):
            out[tile] = total[tile * per + j * 16 : tile * per + j * 16 + 16, :]
        out[8] = jnp.broadcast_to(counts[j * 16 : j * 16 + 16, :], (16, 128))


def final_kernel(mine, core, across, diagonal, centroids, out):
    part = (mine[...] + core[...]) + (across[...] + diagonal[...])
    scale = part[8] + 1.0
    for tile in range(8):
        lanes = slice(tile * 128, tile * 128 + 128)
        out[:, lanes] = (part[tile] + centroids[:, lanes].astype(jnp.float32)) / scale


def call(kernel, outs, vmem, operands, scalars=0, scratch=(), flops=0):
    whole = pl.BlockSpec(memory_space=pltpu.VMEM)
    in_specs = [pl.BlockSpec(memory_space=pltpu.SMEM)] * scalars + [whole] * (len(operands) - scalars)
    return pl.pallas_call(
        kernel,
        out_shape=[jax.ShapeDtypeStruct(shape, dtype) for shape, dtype in outs],
        in_specs=in_specs,
        out_specs=[whole] * len(outs),
        scratch_shapes=scratch,
        compiler_params=pltpu.CompilerParams(vmem_limit_bytes=vmem * MIB),
        cost_estimate=pl.CostEstimate(flops=flops, bytes_accessed=MIB, transcendentals=0),
    )(*operands)


def body(documents, centroids):
    count, width = documents.shape
    beta = 3.0 / math.sqrt(width)
    others = lax.ppermute(documents, "core", SWAP)

    near = [lax.ppermute(centroids, ("zh", "core"), toward(j, 1)) for j in range(2)]
    near = jnp.concatenate(near).reshape(1, 32, width)
    held = lax.all_to_all(
        jnp.broadcast_to(near, (PEERS, 32, width)), ("y", "xh", "zl"), 0, 0, tiled=True
    ).reshape(512, width)

    flops = 2 * 512 * 2 * count * width
    logits, mine = call(
        functools.partial(logits_kernel, beta),
        [((512, 2 * count), jnp.float32), ((4, count), jnp.float32)],
        20,
        (held, documents, others),
        flops=flops,
    )
    theirs = lax.ppermute(mine, "core", SWAP)
    normalizer, packed = call(
        sums_kernel,
        [((1, count), jnp.float32), ((PEERS, 272, 128), jnp.bfloat16)],
        24,
        (logits, mine, theirs, documents, others),
        scratch=[pltpu.VMEM((512, 2 * count), jnp.bfloat16)],
        flops=flops,
    )

    packed = lax.all_to_all(packed, ("y", "xh", "zl"), 0, 0, tiled=True)
    place = (lax.axis_index("y") * 2 + lax.axis_index("xh")) * 2 + lax.axis_index("zl")
    parts = call(
        split_kernel, [((9, 16, 128), jnp.float32)] * 2, 8, (place.reshape(1), packed), scalars=1
    )
    part = sum(lax.ppermute(parts[j], ("zh", "core"), toward(j, -1)) for j in range(2))
    diagonal, across, core = (
        lax.ppermute(part, ("xl", "core"), [(i, i ^ bits) for i in range(4)]) for bits in (3, 2, 1)
    )
    (new_centroids,) = call(
        final_kernel,
        [((16, width), jnp.float32)],
        4,
        (part, core, across, diagonal, centroids),
    )
    return (new_centroids, normalizer.reshape(count))


def solution(mesh):
    fine = Mesh(mesh.devices.reshape(SIZES), AXES)
    in_specs = (P(AXES, None), P(AXES[:4], None))
    out_specs = (P(AXES[:4], None), P(AXES))
    return jax.shard_map(body, mesh=fine, in_specs=in_specs, out_specs=out_specs, check_vma=False)
```

```python
import functools
import math

import jax
import jax.numpy as jnp
from jax import lax
from jax.experimental import pallas as pl
from jax.experimental.pallas import tpu as pltpu
from jax.sharding import PartitionSpec as P

BOTH = ("blk", "dp")
TILE = 512
MIB = 2**20
QUARTERS = [
    [((label - 2 * z) % 4 * 2 + x_hi) * 8 + z for z in range(8) for x_hi in range(2)] for label in range(4)
]


def star(side, sign):
    found = []
    for source in range(256):
        blk, dp = divmod(source, 4)
        y, x_hi, z = blk // 16, blk // 8 % 2, blk % 8
        if side == 2:
            z = (z + sign * (1 - 2 * (dp % 2))) % 8
        else:
            y = (y + sign * (1 - 2 * side)) % 4
        found.append((source, ((y * 2 + x_hi) * 8 + z) * 4 + dp))
    return found


def within(bits):
    return [(i, i ^ bits) for i in range(4)]


def turn_kernel(source, out):
    for start in range(0, source.shape[0], TILE):
        out[:, start : start + TILE] = source[start : start + TILE, :].T


def logits_kernel(beta, old, *refs):
    *refs, logits, stats, held = refs
    before, refs = refs[:old], refs[old:]
    *quarters, docs, others = refs
    count = docs.shape[1]
    for i, quarter in enumerate(quarters):
        held[i * 128 : i * 128 + 128, :] = quarter[...]
    block = held[...]
    wide = block.astype(jnp.float32)
    shift = (0.5 * beta) * jnp.sum(wide * wide, axis=1, keepdims=True)
    for side, source in enumerate((docs, others)):
        for start in range(0, count, TILE):
            columns = slice(start, start + TILE)
            part = jnp.dot(block, source[:, columns], preferred_element_type=jnp.float32)
            part = beta * part - shift
            logits[:, side * count + start : side * count + start + TILE] = part
            top = jnp.max(part, axis=0, keepdims=True)
            for stat in before:
                top = jnp.maximum(top, stat[side : side + 1, columns])
            total = jnp.sum(jnp.exp(part - top), axis=0, keepdims=True)
            for stat in before:
                total += stat[2 + side : 3 + side, columns] * jnp.exp(stat[side : side + 1, columns] - top)
            stats[side : side + 1, columns] = top
            stats[2 + side : 3 + side, columns] = total


def two_rows(counts):
    high = counts.astype(jnp.bfloat16)
    rest = (counts - high.astype(jnp.float32)).astype(jnp.bfloat16)
    return jnp.concatenate([high, rest, jnp.zeros((14, 128), jnp.bfloat16)], axis=0)


def write_sums(low, docs, others, rows, counts, outs):
    count = docs.shape[0]
    for i, out in enumerate(outs):
        row = counts[i : i + 1, :]
        if out.dtype == jnp.float32:
            out[1024:1032, :] = jnp.broadcast_to(row, (8, 128))
        else:
            out[1024:1040, :] = two_rows(row)
    for start in range(0, docs.shape[1], 256):
        columns = slice(start, start + 256)
        sums = jnp.dot(low[rows, :count], docs[:, columns], preferred_element_type=jnp.float32)
        sums += jnp.dot(low[rows, count:], others[:, columns], preferred_element_type=jnp.float32)
        for i, out in enumerate(outs):
            for half in range(2):
                part = sums[i * 128 : i * 128 + 128, half * 128 : half * 128 + 128]
                out[start + half * 128 : start + half * 128 + 128, :] = part.astype(out.dtype)


def weights_kernel(first, second, mine, theirs, docs, others, normalizer, low, rest, up, down):
    count = docs.shape[0]
    counts = jnp.zeros((512, 128), jnp.float32)
    for side in range(2):
        a, b = mine[side : side + 1, :], theirs[1 - side : 2 - side, :]
        top = jnp.maximum(a, b)
        total = mine[2 + side : 3 + side, :] * jnp.exp(a - top)
        total += theirs[3 - side : 4 - side, :] * jnp.exp(b - top)
        norm = top + jnp.log(total)
        if side == 0:
            normalizer[...] = norm
        for start in range(0, count, TILE):
            at = slice(side * count + start, side * count + start + TILE)
            logits = jnp.concatenate([second[:, at], first[:, at]], axis=0)
            weights = jnp.exp(logits - norm[:, start : start + TILE])
            for k in range(0, TILE, 128):
                counts += weights[:, k : k + 128]
            low[:, at] = weights.astype(jnp.bfloat16)
    flat = jnp.sum(counts.T, axis=0, keepdims=True)
    flat = jnp.concatenate([flat[:, i : i + 128] for i in range(0, 512, 128)], axis=0)
    rest[...] = flat[2:4, :]
    write_sums(low, docs, others, slice(0, 256), flat, (up, down))


def rest_kernel(low, counts, docs, others, deep, own):
    write_sums(low, docs, others, slice(256, 512), counts, (deep, own))


def star_kernel(own, up, down, deep, packed):
    counts = own[1024:1025, :]
    for part in (up, down, deep):
        rows = part[1024:1040, :].astype(jnp.float32)
        counts = counts + (rows[0:1, :] + rows[1:2, :])

    def total(tile):
        rows = slice(tile * 128, tile * 128 + 128)
        left = own[rows, :] + up[rows, :].astype(jnp.float32)
        right = down[rows, :].astype(jnp.float32) + deep[rows, :].astype(jnp.float32)
        return (left + right).reshape(16, 8, 128)

    for tile in range(0, 8, 2):
        pair = jnp.concatenate([total(tile), total(tile + 1)], axis=1)
        packed[:, tile * 8 : tile * 8 + 16, :] = pair.astype(jnp.bfloat16)
    slab = two_rows(counts)
    for member in range(16):
        packed[member, 64:80, :] = slab


def group_kernel(place, packed, out):
    total = jnp.sum(packed[...].astype(jnp.float32), axis=0)
    for tile in range(8):
        out[tile] = total[tile * 8 : tile * 8 + 8, :]
    lane = lax.broadcasted_iota(jnp.int32, (8, 128), 1)
    wanted = lax.broadcasted_iota(jnp.int32, (8, 128), 0) + place[0] * 8
    counts = jnp.where(lane == wanted, total[64:65, :] + total[65:66, :], 0.0)
    out[8] = jnp.broadcast_to(jnp.sum(counts, axis=1, keepdims=True), (8, 128))


def final_kernel(core, mine, swapped, across, diagonal, centroids, out):
    same = mine[...] + across[...]
    far = swapped[...] + diagonal[...]
    first = core[0] == 0
    for half, part in enumerate((jnp.where(first, same, far), jnp.where(first, far, same))):
        scale = part[8] + 1.0
        for tile in range(8):
            lanes = slice(tile * 128, tile * 128 + 128)
            held = centroids[:, lanes].astype(jnp.float32)[half * 8 : half * 8 + 8, :]
            out[half * 8 : half * 8 + 8, lanes] = (part[tile] + held) / scale


def call(kernel, outs, vmem, operands, scalars=0, scratch=(), flops=0):
    whole = pl.BlockSpec(memory_space=pltpu.VMEM)
    return pl.pallas_call(
        kernel,
        out_shape=[jax.ShapeDtypeStruct(shape, dtype) for shape, dtype in outs],
        in_specs=[pl.BlockSpec(memory_space=pltpu.SMEM)] * scalars + [whole] * (len(operands) - scalars),
        out_specs=[whole] * len(outs),
        scratch_shapes=scratch,
        compiler_params=pltpu.CompilerParams(vmem_limit_bytes=vmem * MIB),
        cost_estimate=pl.CostEstimate(flops=flops, bytes_accessed=MIB, transcendentals=0),
    )(*operands)


def exchange(part):
    return lax.all_to_all(part, "blk", 0, 0, axis_index_groups=QUARTERS, tiled=True)


def body(documents, centroids):
    count, width = documents.shape
    beta = 3.0 / math.sqrt(width)
    blk = lax.axis_index("blk")
    core = lax.axis_index("dp") % 2
    others = lax.ppermute(documents, "dp", within(1))

    near = lax.dynamic_slice_in_dim(centroids, core * 8, 8, 0).reshape(1, 8, width)
    quarter = exchange(jnp.broadcast_to(near, (16, 8, width))).reshape(128, width)
    quarters = [quarter] + [lax.ppermute(quarter, BOTH, star(side, -1)) for side in range(3)]

    flops = 2 * 512 * 2 * count * width
    turned = [
        call(turn_kernel, [((width, count), jnp.bfloat16)], 10, (part,), flops=flops // 2)[0]
        for part in (documents, others)
    ]
    first, stats = call(
        functools.partial(logits_kernel, beta, 0),
        [((128, 2 * count), jnp.float32), ((4, count), jnp.float32)],
        12,
        (quarters[0], *turned),
        scratch=[pltpu.VMEM((128, width), jnp.bfloat16)],
        flops=flops // 2,
    )
    second, mine = call(
        functools.partial(logits_kernel, beta, 1),
        [((384, 2 * count), jnp.float32), ((4, count), jnp.float32)],
        16,
        (stats, *quarters[1:], *turned),
        scratch=[pltpu.VMEM((384, width), jnp.bfloat16)],
        flops=flops,
    )
    theirs = lax.ppermute(mine, "dp", within(1))
    slab = ((1040, 128), jnp.bfloat16)
    normalizer, low, counts, up, down = call(
        weights_kernel,
        [((1, count), jnp.float32), ((512, 2 * count), jnp.bfloat16), ((2, 128), jnp.float32), slab, slab],
        24,
        (first, second, mine, theirs, documents, others),
        flops=flops,
    )
    deep, own = call(
        rest_kernel, [slab, ((1032, 128), jnp.float32)], 16, (low, counts, documents, others), flops=flops // 2
    )
    sent = (up, down, deep)

    came = [lax.ppermute(part, BOTH, star(side, 1)) for side, part in enumerate(sent)]
    (packed,) = call(star_kernel, [((16, 80, 128), jnp.bfloat16)], 8, (own, *came))
    place = blk % 8 * 2 + blk // 8 % 2
    (part,) = call(
        group_kernel, [((9, 8, 128), jnp.float32)], 4, (place.reshape(1), exchange(packed)), scalars=1
    )
    diagonal, across, swapped = (lax.ppermute(part, "dp", within(bits)) for bits in (3, 2, 1))
    (new_centroids,) = call(
        final_kernel,
        [((16, width), jnp.float32)],
        4,
        (core.reshape(1), part, swapped, across, diagonal, centroids),
        scalars=1,
    )
    return (new_centroids, normalizer.reshape(count))


def solution(mesh):
    in_specs = (P(BOTH, None), P("blk", None))
    out_specs = (P("blk", None), P(BOTH))
    return jax.shard_map(body, mesh=mesh, in_specs=in_specs, out_specs=out_specs, check_vma=False)
```

```python
import functools
import math

import jax
import jax.numpy as jnp
from jax import lax
from jax.experimental import pallas as pl
from jax.experimental.pallas import tpu as pltpu
from jax.sharding import PartitionSpec as P

BOTH = ("blk", "dp")
TILE = 512
MIB = 2**20
FIRST = (5, 5, 4, 4)
GROUPS = [
    [
        (((label - 2 * z) % 4 * 2 + x_hi) * 8 + z % 8) * 4 + (x_hi ^ flip) * 2 + core
        for z in range(FIRST[label], FIRST[label] + 8)
        for x_hi in (1, 0)
    ]
    for label in range(4)
    for flip in range(2)
    for core in range(2)
]

TURN = 0


def star(side, sign):
    found = []
    for source in range(256):
        blk, dp = divmod(source, 4)
        y, x_hi, z = blk // 16, blk // 8 % 2, blk % 8
        if side == 2:
            z = (z + sign * (1 - 2 * (dp % 2))) % 8
        else:
            y = (y + sign * (1 - 2 * side)) % 4
        found.append((source, ((y * 2 + x_hi) * 8 + z) * 4 + dp))
    return found


def within(bits):
    return [(i, i ^ bits) for i in range(4)]


def repeat_kernel(core, centroids, out):
    whole = centroids[...].astype(jnp.float32)
    half = jnp.where(core[0] == 0, whole[:8, :], whole[8:, :])
    twice = jnp.concatenate([half, half], axis=0).astype(jnp.bfloat16)
    for start in range(0, 128, 16):
        out[start : start + 16, :] = twice


def turn_kernel(source, out):
    for start in range(0, source.shape[0], TILE):
        out[:, start : start + TILE] = source[start : start + TILE, :].T


def logits_kernel(beta, old, *refs):
    *refs, logits, stats, held = refs
    before, refs = refs[:old], refs[old:]
    *quarters, docs, others = refs
    count = docs.shape[1]
    for i, quarter in enumerate(quarters):
        held[i * 128 : i * 128 + 128, :] = quarter[...]
    block = held[...]
    wide = block.astype(jnp.float32)
    shift = (0.5 * beta) * jnp.sum(wide * wide, axis=1, keepdims=True)
    for side, source in enumerate((docs, others)):
        for start in range(0, count, TILE):
            columns = slice(start, start + TILE)
            part = jnp.dot(block, source[:, columns], preferred_element_type=jnp.float32)
            part = beta * part - shift
            logits[:, side * count + start : side * count + start + TILE] = part
            top = jnp.max(part, axis=0, keepdims=True)
            for stat in before:
                top = jnp.maximum(top, stat[side : side + 1, columns])
            total = jnp.sum(jnp.exp(part - top), axis=0, keepdims=True)
            for stat in before:
                total += stat[2 + side : 3 + side, columns] * jnp.exp(stat[side : side + 1, columns] - top)
            stats[side : side + 1, columns] = top
            stats[2 + side : 3 + side, columns] = total


def two_rows(counts):
    high = counts.astype(jnp.bfloat16)
    rest = (counts - high.astype(jnp.float32)).astype(jnp.bfloat16)
    return jnp.concatenate([high, rest, jnp.zeros((14, 128), jnp.bfloat16)], axis=0)


def write_sums(low, docs, others, rows, counts, outs):
    count = docs.shape[0]
    for i, out in enumerate(outs):
        row = counts[i : i + 1, :]
        if out.dtype == jnp.float32:
            out[1024:1032, :] = jnp.broadcast_to(row, (8, 128))
        else:
            out[1024:1040, :] = two_rows(row)
    for start in range(0, docs.shape[1], 256):
        columns = slice(start, start + 256)
        sums = jnp.dot(low[rows, :count], docs[:, columns], preferred_element_type=jnp.float32)
        sums += jnp.dot(low[rows, count:], others[:, columns], preferred_element_type=jnp.float32)
        for i, out in enumerate(outs):
            for half in range(2):
                part = sums[i * 128 : i * 128 + 128, half * 128 : half * 128 + 128]
                out[start + half * 128 : start + half * 128 + 128, :] = part.astype(out.dtype)


def weights_kernel(pair, deep, own, mine, theirs, docs, others, normalizer, low, rest, up, down):
    count = docs.shape[0]
    counts = jnp.zeros((512, 128), jnp.float32)
    for side in range(2):
        a, b = mine[side : side + 1, :], theirs[1 - side : 2 - side, :]
        top = jnp.maximum(a, b)
        total = mine[2 + side : 3 + side, :] * jnp.exp(a - top)
        total += theirs[3 - side : 4 - side, :] * jnp.exp(b - top)
        norm = top + jnp.log(total)
        if side == 0:
            normalizer[...] = norm
        for start in range(0, count, TILE):
            at = slice(side * count + start, side * count + start + TILE)
            logits = jnp.concatenate([pair[:, at], deep[:, at], own[:, at]], axis=0)
            weights = jnp.exp(logits - norm[:, start : start + TILE])
            for k in range(0, TILE, 128):
                counts += weights[:, k : k + 128]
            low[:, at] = weights.astype(jnp.bfloat16)
    flat = jnp.sum(counts.T, axis=0, keepdims=True)
    flat = jnp.concatenate([flat[:, i : i + 128] for i in range(0, 512, 128)], axis=0)
    rest[...] = flat[2:4, :]
    write_sums(low, docs, others, slice(0, 256), flat, (up, down))


def rest_kernel(index, low, counts, docs, others, out):
    rows = slice(256 + 128 * index, 384 + 128 * index)
    write_sums(low, docs, others, rows, counts[index : index + 1, :], (out,))


def star_kernel(own, up, down, deep, packed):
    counts = own[1024:1025, :]
    for part in (up, down, deep):
        rows = part[1024:1040, :].astype(jnp.float32)
        counts = counts + (rows[0:1, :] + rows[1:2, :])

    def total(tile):
        rows = slice(tile * 128, tile * 128 + 128)
        left = own[rows, :] + up[rows, :].astype(jnp.float32)
        right = down[rows, :].astype(jnp.float32) + deep[rows, :].astype(jnp.float32)
        result = (left + right).reshape(16, 8, 128)
        return jnp.concatenate([result[TURN:], result[:TURN]], axis=0) if TURN else result

    for tile in range(0, 8, 2):
        pair = jnp.concatenate([total(tile), total(tile + 1)], axis=1)
        packed[:, tile * 8 : tile * 8 + 16, :] = pair.astype(jnp.bfloat16)
    slab = two_rows(counts)
    for member in range(16):
        packed[member, 64:80, :] = slab


def group_kernel(place, packed, out):
    total = jnp.sum(packed[...].astype(jnp.float32), axis=0)
    for tile in range(8):
        out[tile] = total[tile * 8 : tile * 8 + 8, :]
    lane = lax.broadcasted_iota(jnp.int32, (8, 128), 1)
    wanted = lax.broadcasted_iota(jnp.int32, (8, 128), 0) + place[0] * 8
    counts = jnp.where(lane == wanted, total[64:65, :] + total[65:66, :], 0.0)
    out[8] = jnp.broadcast_to(jnp.sum(counts, axis=1, keepdims=True), (8, 128))


def finish_kernel(core, mine, across, centroids, out):
    part = mine[...] + across[...]
    scale = part[8] + 1.0
    for tile in range(8):
        lanes = slice(tile * 128, tile * 128 + 128)
        held = centroids[:, lanes].astype(jnp.float32)
        held = jnp.where(core[0] == 0, held[:8, :], held[8:, :])
        out[:, lanes] = (part[tile] + held) / scale


def join_kernel(core, mine, other, out):
    first = core[0] == 0
    out[:8, :] = jnp.where(first, mine[...], other[...])
    out[8:, :] = jnp.where(first, other[...], mine[...])


def call(kernel, outs, vmem, operands, scalars=0, scratch=(), flops=0):
    whole = pl.BlockSpec(memory_space=pltpu.VMEM)
    return pl.pallas_call(
        kernel,
        out_shape=[jax.ShapeDtypeStruct(shape, dtype) for shape, dtype in outs],
        in_specs=[pl.BlockSpec(memory_space=pltpu.SMEM)] * scalars + [whole] * (len(operands) - scalars),
        out_specs=[whole] * len(outs),
        scratch_shapes=scratch,
        compiler_params=pltpu.CompilerParams(vmem_limit_bytes=vmem * MIB),
        cost_estimate=pl.CostEstimate(flops=flops, bytes_accessed=MIB, transcendentals=0),
    )(*operands)


def exchange(part, turn=0):
    groups = [group[turn:] + group[:turn] for group in GROUPS]
    return lax.all_to_all(part, BOTH, 0, 0, axis_index_groups=groups, tiled=True)


def body(documents, centroids):
    count, width = documents.shape
    beta = 3.0 / math.sqrt(width)
    blk = lax.axis_index("blk")
    core = lax.axis_index("dp") % 2
    others = lax.ppermute(documents, "dp", within(1))

    near = lax.dynamic_slice_in_dim(centroids, core * 8, 8, 0).reshape(1, 8, width)
    quarter = exchange(jnp.broadcast_to(near, (16, 8, width))).reshape(128, width)
    quarters = [quarter] + [lax.ppermute(quarter, BOTH, star(side, -1)) for side in range(3)]

    flops = 2 * 512 * 2 * count * width
    turned = [
        call(turn_kernel, [((width, count), jnp.bfloat16)], 10, (part,), flops=flops // 2)[0]
        for part in (documents, others)
    ]
    own, up, down, deep = quarters
    logits, stats = [], []
    for held in ((own,), (deep,), (up, down)):
        rows = 128 * len(held)
        part, stat = call(
            functools.partial(logits_kernel, beta, len(stats[-1:])),
            [((rows, 2 * count), jnp.float32), ((4, count), jnp.float32)],
            14,
            (*stats[-1:], *held, *turned),
            scratch=[pltpu.VMEM((rows, width), jnp.bfloat16)],
            flops=flops * rows // 512 // 8,
        )
        logits.append(part)
        stats.append(stat)
    mine = stats[-1]
    theirs = lax.ppermute(mine, "dp", within(1))
    slab = ((1040, 128), jnp.bfloat16)
    normalizer, low, counts, up, down = call(
        weights_kernel,
        [((1, count), jnp.float32), ((512, 2 * count), jnp.bfloat16), ((2, 128), jnp.float32), slab, slab],
        24,
        (*logits[::-1], mine, theirs, documents, others),
        flops=flops,
    )
    (deep,), (own,) = (
        call(
            functools.partial(rest_kernel, index),
            [out],
            16,
            (low, counts, documents, others),
            flops=flops // 64,
        )
        for index, out in enumerate((slab, ((1032, 128), jnp.float32)))
    )
    sent = (up, down, deep)

    came = [lax.ppermute(part, BOTH, star(side, 1)) for side, part in enumerate(sent)]
    (packed,) = call(star_kernel, [((16, 80, 128), jnp.bfloat16)], 8, (own, *came))
    label = (blk // 16 + 2 * blk) % 4
    place = (blk - jnp.asarray(FIRST)[label]) % 8 * 2 + 1 - blk // 8 % 2
    (part,) = call(
        group_kernel, [((9, 8, 128), jnp.float32)], 4, (place.reshape(1), exchange(packed, TURN)), scalars=1
    )
    across = lax.ppermute(part, "dp", within(2))
    (half,) = call(
        finish_kernel,
        [((8, width), jnp.float32)],
        4,
        (core.reshape(1), part, across, centroids),
        scalars=1,
    )
    other = lax.ppermute(half, "dp", within(1))
    (new_centroids,) = call(
        join_kernel, [((16, width), jnp.float32)], 4, (core.reshape(1), half, other), scalars=1
    )
    return (new_centroids, normalizer.reshape(count))


def solution(mesh):
    in_specs = (P(BOTH, None), P("blk", None))
    out_specs = (P("blk", None), P(BOTH))
    return jax.shard_map(body, mesh=mesh, in_specs=in_specs, out_specs=out_specs, check_vma=False)
```

```python
import functools
import math

import jax
import jax.numpy as jnp
from jax import lax
from jax.experimental import pallas as pl
from jax.experimental.pallas import tpu as pltpu
from jax.sharding import PartitionSpec as P

BOTH = ("blk", "dp")
TILE = 512
MIB = 2**20
FIRST = (5, 5, 4, 4)
GROUPS = [
    [
        (((label - 2 * z) % 4 * 2 + x_hi) * 8 + z % 8) * 4 + (x_hi ^ flip) * 2 + core
        for z in range(FIRST[label], FIRST[label] + 8)
        for x_hi in (1, 0)
    ]
    for label in range(4)
    for flip in range(2)
    for core in range(2)
]

TURN = 0


def star(side, sign):
    found = []
    for source in range(256):
        blk, dp = divmod(source, 4)
        y, x_hi, z = blk // 16, blk // 8 % 2, blk % 8
        if side == 2:
            z = (z + sign * (1 - 2 * (dp % 2))) % 8
        else:
            y = (y + sign * (1 - 2 * side)) % 4
        found.append((source, ((y * 2 + x_hi) * 8 + z) * 4 + dp))
    return found


def within(bits):
    return [(i, i ^ bits) for i in range(4)]


def repeat_kernel(core, centroids, out):
    whole = centroids[...].astype(jnp.float32)
    half = jnp.where(core[0] == 0, whole[:8, :], whole[8:, :])
    twice = jnp.concatenate([half, half], axis=0).astype(jnp.bfloat16)
    for start in range(0, 128, 16):
        out[start : start + 16, :] = twice


def turn_kernel(source, out):
    for start in range(0, source.shape[0], TILE):
        out[:, start : start + TILE] = source[start : start + TILE, :].T


def logits_kernel(beta, old, *refs):
    *refs, logits, stats, held = refs
    before, refs = refs[:old], refs[old:]
    *quarters, docs, others = refs
    count = docs.shape[1]
    for i, quarter in enumerate(quarters):
        held[i * 128 : i * 128 + 128, :] = quarter[...]
    block = held[...]
    wide = block.astype(jnp.float32)
    shift = (0.5 * beta) * jnp.sum(wide * wide, axis=1, keepdims=True)
    for side, source in enumerate((docs, others)):
        for start in range(0, count, TILE):
            columns = slice(start, start + TILE)
            part = jnp.dot(block, source[:, columns], preferred_element_type=jnp.float32)
            part = beta * part - shift
            logits[:, side * count + start : side * count + start + TILE] = part
            top = jnp.max(part, axis=0, keepdims=True)
            for stat in before:
                top = jnp.maximum(top, stat[side : side + 1, columns])
            total = jnp.sum(jnp.exp(part - top), axis=0, keepdims=True)
            for stat in before:
                total += stat[2 + side : 3 + side, columns] * jnp.exp(stat[side : side + 1, columns] - top)
            stats[side : side + 1, columns] = top
            stats[2 + side : 3 + side, columns] = total


def two_rows(counts):
    high = counts.astype(jnp.bfloat16)
    rest = (counts - high.astype(jnp.float32)).astype(jnp.bfloat16)
    return jnp.concatenate([high, rest, jnp.zeros((14, 128), jnp.bfloat16)], axis=0)


def write_sums(low, docs, others, rows, counts, outs):
    count = docs.shape[0]
    for i, out in enumerate(outs):
        row = counts[i : i + 1, :]
        if out.dtype == jnp.float32:
            out[1024:1032, :] = jnp.broadcast_to(row, (8, 128))
        else:
            out[1024:1040, :] = two_rows(row)
    for start in range(0, docs.shape[1], 256):
        columns = slice(start, start + 256)
        sums = jnp.dot(low[rows, :count], docs[:, columns], preferred_element_type=jnp.float32)
        sums += jnp.dot(low[rows, count:], others[:, columns], preferred_element_type=jnp.float32)
        for i, out in enumerate(outs):
            for half in range(2):
                part = sums[i * 128 : i * 128 + 128, half * 128 : half * 128 + 128]
                out[start + half * 128 : start + half * 128 + 128, :] = part.astype(out.dtype)


def weights_kernel(pair, deep, own, mine, theirs, docs, others, normalizer, low, rest, up, down, third):
    count = docs.shape[0]
    counts = jnp.zeros((512, 128), jnp.float32)
    for side in range(2):
        a, b = mine[side : side + 1, :], theirs[1 - side : 2 - side, :]
        top = jnp.maximum(a, b)
        total = mine[2 + side : 3 + side, :] * jnp.exp(a - top)
        total += theirs[3 - side : 4 - side, :] * jnp.exp(b - top)
        norm = top + jnp.log(total)
        if side == 0:
            normalizer[...] = norm
        for start in range(0, count, TILE):
            at = slice(side * count + start, side * count + start + TILE)
            logits = jnp.concatenate([pair[:, at], deep[:, at], own[:, at]], axis=0)
            weights = jnp.exp(logits - norm[:, start : start + TILE])
            for k in range(0, TILE, 128):
                counts += weights[:, k : k + 128]
            low[:, at] = weights.astype(jnp.bfloat16)
    flat = jnp.sum(counts.T, axis=0, keepdims=True)
    flat = jnp.concatenate([flat[:, i : i + 128] for i in range(0, 512, 128)], axis=0)
    rest[...] = flat[3:4, :]
    write_sums(low, docs, others, slice(0, 384), flat, (up, down, third))


def rest_kernel(low, counts, docs, others, own):
    write_sums(low, docs, others, slice(384, 512), counts, (own,))


def star_kernel(own, up, down, deep, packed):
    counts = own[1024:1025, :]
    for part in (up, down, deep):
        rows = part[1024:1040, :].astype(jnp.float32)
        counts = counts + (rows[0:1, :] + rows[1:2, :])

    def total(tile):
        rows = slice(tile * 128, tile * 128 + 128)
        left = own[rows, :] + up[rows, :].astype(jnp.float32)
        right = down[rows, :].astype(jnp.float32) + deep[rows, :].astype(jnp.float32)
        result = (left + right).reshape(16, 8, 128)
        return jnp.concatenate([result[TURN:], result[:TURN]], axis=0) if TURN else result

    for tile in range(0, 8, 2):
        pair = jnp.concatenate([total(tile), total(tile + 1)], axis=1)
        packed[:, tile * 8 : tile * 8 + 16, :] = pair.astype(jnp.bfloat16)
    slab = two_rows(counts)
    for member in range(16):
        packed[member, 64:80, :] = slab


def group_kernel(place, packed, out):
    total = jnp.sum(packed[...].astype(jnp.float32), axis=0)
    for tile in range(8):
        out[tile] = total[tile * 8 : tile * 8 + 8, :]
    lane = lax.broadcasted_iota(jnp.int32, (8, 128), 1)
    wanted = lax.broadcasted_iota(jnp.int32, (8, 128), 0) + place[0] * 8
    counts = jnp.where(lane == wanted, total[64:65, :] + total[65:66, :], 0.0)
    out[8] = jnp.broadcast_to(jnp.sum(counts, axis=1, keepdims=True), (8, 128))


def finish_kernel(core, mine, across, centroids, out):
    part = mine[...] + across[...]
    scale = part[8] + 1.0
    for tile in range(8):
        lanes = slice(tile * 128, tile * 128 + 128)
        held = centroids[:, lanes].astype(jnp.float32)
        held = jnp.where(core[0] == 0, held[:8, :], held[8:, :])
        out[:, lanes] = (part[tile] + held) / scale


def join_kernel(core, mine, other, out):
    first = core[0] == 0
    out[:8, :] = jnp.where(first, mine[...], other[...])
    out[8:, :] = jnp.where(first, other[...], mine[...])


def call(kernel, outs, vmem, operands, scalars=0, scratch=(), flops=0):
    whole = pl.BlockSpec(memory_space=pltpu.VMEM)
    return pl.pallas_call(
        kernel,
        out_shape=[jax.ShapeDtypeStruct(shape, dtype) for shape, dtype in outs],
        in_specs=[pl.BlockSpec(memory_space=pltpu.SMEM)] * scalars + [whole] * (len(operands) - scalars),
        out_specs=[whole] * len(outs),
        scratch_shapes=scratch,
        compiler_params=pltpu.CompilerParams(vmem_limit_bytes=vmem * MIB),
        cost_estimate=pl.CostEstimate(flops=flops, bytes_accessed=MIB, transcendentals=0),
    )(*operands)


def exchange(part, turn=0):
    groups = [group[turn:] + group[:turn] for group in GROUPS]
    return lax.all_to_all(part, BOTH, 0, 0, axis_index_groups=groups, tiled=True)


def body(documents, centroids):
    count, width = documents.shape
    beta = 3.0 / math.sqrt(width)
    blk = lax.axis_index("blk")
    core = lax.axis_index("dp") % 2
    others = lax.ppermute(documents, "dp", within(1))

    near = lax.dynamic_slice_in_dim(centroids, core * 8, 8, 0).reshape(1, 8, width)
    quarter = exchange(jnp.broadcast_to(near, (16, 8, width))).reshape(128, width)
    quarters = [quarter] + [lax.ppermute(quarter, BOTH, star(side, -1)) for side in range(3)]

    flops = 2 * 512 * 2 * count * width
    turned = [
        call(turn_kernel, [((width, count), jnp.bfloat16)], 10, (part,), flops=flops // 64)[0]
        for part in (documents, others)
    ]
    own, up, down, deep = quarters
    logits, stats = [], []
    for held in ((own,), (deep,), (up, down)):
        rows = 128 * len(held)
        part, stat = call(
            functools.partial(logits_kernel, beta, len(stats[-1:])),
            [((rows, 2 * count), jnp.float32), ((4, count), jnp.float32)],
            14,
            (*stats[-1:], *held, *turned),
            scratch=[pltpu.VMEM((rows, width), jnp.bfloat16)],
            flops=flops * rows // 512 // 8,
        )
        logits.append(part)
        stats.append(stat)
    mine = stats[-1]
    theirs = lax.ppermute(mine, "dp", within(1))
    slab = ((1040, 128), jnp.bfloat16)
    normalizer, low, counts, up, down, deep = call(
        weights_kernel,
        [((1, count), jnp.float32), ((512, 2 * count), jnp.bfloat16), ((1, 128), jnp.float32), slab, slab, slab],
        24,
        (*logits[::-1], mine, theirs, documents, others),
        flops=flops,
    )
    (own,) = call(
        rest_kernel, [((1032, 128), jnp.float32)], 16, (low, counts, documents, others), flops=flops // 4
    )
    sent = (up, down, deep)

    came = [lax.ppermute(part, BOTH, star(side, 1)) for side, part in enumerate(sent)]
    (packed,) = call(star_kernel, [((16, 80, 128), jnp.bfloat16)], 8, (own, *came))
    label = (blk // 16 + 2 * blk) % 4
    place = (blk - jnp.asarray(FIRST)[label]) % 8 * 2 + 1 - blk // 8 % 2
    (part,) = call(
        group_kernel, [((9, 8, 128), jnp.float32)], 4, (place.reshape(1), exchange(packed, TURN)), scalars=1
    )
    across = lax.ppermute(part, "dp", within(2))
    (half,) = call(
        finish_kernel,
        [((8, width), jnp.float32)],
        4,
        (core.reshape(1), part, across, centroids),
        scalars=1,
    )
    other = lax.ppermute(half, "dp", within(1))
    (new_centroids,) = call(
        join_kernel, [((16, width), jnp.float32)], 4, (core.reshape(1), half, other), scalars=1
    )
    return (new_centroids, normalizer.reshape(count))


def solution(mesh):
    in_specs = (P(BOTH, None), P("blk", None))
    out_specs = (P("blk", None), P(BOTH))
    return jax.shard_map(body, mesh=mesh, in_specs=in_specs, out_specs=out_specs, check_vma=False)
```

```python
import functools
import math

import jax
import jax.numpy as jnp
from jax import lax
from jax.experimental import pallas as pl
from jax.experimental.pallas import tpu as pltpu
from jax.sharding import PartitionSpec as P

BOTH = ("blk", "dp")
TILE = 512
MIB = 2**20
FIRST = (5, 5, 4, 4)
GROUPS = [
    [
        (((label - 2 * z) % 4 * 2 + x_hi) * 8 + z % 8) * 4 + (x_hi ^ flip) * 2 + core
        for z in range(FIRST[label], FIRST[label] + 8)
        for x_hi in (1, 0)
    ]
    for label in range(4)
    for flip in range(2)
    for core in range(2)
]


def star(side, sign):
    found = []
    for source in range(256):
        blk, dp = divmod(source, 4)
        y, x_hi, z = blk // 16, blk // 8 % 2, blk % 8
        if side == 2:
            z = (z + sign * (1 - 2 * (dp % 2))) % 8
        else:
            y = (y + sign * (1 - 2 * side)) % 4
        found.append((source, ((y * 2 + x_hi) * 8 + z) * 4 + dp))
    return found


def within(bits):
    return [(i, i ^ bits) for i in range(4)]


def turn_kernel(source, out):
    for start in range(0, source.shape[0], TILE):
        out[:, start : start + TILE] = source[start : start + TILE, :].T


def logits_kernel(beta, old, *refs):
    *refs, logits, stats, held = refs
    before, refs = refs[:old], refs[old:]
    *quarters, docs, others = refs
    count = docs.shape[1]
    for i, quarter in enumerate(quarters):
        held[i * 128 : i * 128 + 128, :] = quarter[...]
    block = held[...]
    wide = block.astype(jnp.float32)
    shift = (0.5 * beta) * jnp.sum(wide * wide, axis=1, keepdims=True)
    for side, source in enumerate((docs, others)):
        for start in range(0, count, TILE):
            columns = slice(start, start + TILE)
            part = jnp.dot(block, source[:, columns], preferred_element_type=jnp.float32)
            part = beta * part - shift
            logits[:, side * count + start : side * count + start + TILE] = part
            top = jnp.max(part, axis=0, keepdims=True)
            for stat in before:
                top = jnp.maximum(top, stat[side : side + 1, columns])
            total = jnp.sum(jnp.exp(part - top), axis=0, keepdims=True)
            for stat in before:
                total += stat[2 + side : 3 + side, columns] * jnp.exp(stat[side : side + 1, columns] - top)
            stats[side : side + 1, columns] = top
            stats[2 + side : 3 + side, columns] = total


def two_rows(counts):
    high = counts.astype(jnp.bfloat16)
    rest = (counts - high.astype(jnp.float32)).astype(jnp.bfloat16)
    return jnp.concatenate([high, rest, jnp.zeros((14, 128), jnp.bfloat16)], axis=0)


def write_sums(low, docs, others, counts, outs):
    count = docs.shape[0]
    for i, out in enumerate(outs):
        row = counts[i : i + 1, :]
        if out.dtype == jnp.float32:
            out[1024:1032, :] = jnp.broadcast_to(row, (8, 128))
        else:
            out[1024:1040, :] = two_rows(row)
    for start in range(0, docs.shape[1], 256):
        columns = slice(start, start + 256)
        sums = jnp.dot(low[:, :count], docs[:, columns], preferred_element_type=jnp.float32)
        sums += jnp.dot(low[:, count:], others[:, columns], preferred_element_type=jnp.float32)
        for i, out in enumerate(outs):
            for half in range(2):
                part = sums[i * 128 : i * 128 + 128, half * 128 : half * 128 + 128]
                out[start + half * 128 : start + half * 128 + 128, :] = part.astype(out.dtype)


def weigh(logits, norms, low):
    count = norms.shape[1]
    counts = jnp.zeros((low.shape[0], 128), jnp.float32)
    for side in range(2):
        for start in range(0, count, TILE):
            at = slice(side * count + start, side * count + start + TILE)
            part = jnp.concatenate([ref[:, at] for ref in logits], axis=0)
            weights = jnp.exp(part - norms[side : side + 1, start : start + TILE])
            for k in range(0, TILE, 128):
                counts += weights[:, k : k + 128]
            low[:, at] = weights.astype(jnp.bfloat16)
    flat = jnp.sum(counts.T, axis=0, keepdims=True)
    return jnp.concatenate([flat[:, i : i + 128] for i in range(0, flat.shape[1], 128)], axis=0)


def sent_kernel(pair, deep, mine, theirs, docs, others, normalizer, norms, *refs):
    *outs, low = refs
    for side in range(2):
        a, b = mine[side : side + 1, :], theirs[1 - side : 2 - side, :]
        top = jnp.maximum(a, b)
        total = mine[2 + side : 3 + side, :] * jnp.exp(a - top)
        total += theirs[3 - side : 4 - side, :] * jnp.exp(b - top)
        norms[side : side + 1, :] = top + jnp.log(total)
    normalizer[...] = norms[0:1, :]
    write_sums(low, docs, others, weigh((pair, deep), norms, low), outs)


def own_kernel(own, norms, docs, others, out, low):
    write_sums(low, docs, others, weigh((own,), norms, low), (out,))


def star_kernel(own, up, down, deep, packed):
    counts = own[1024:1025, :]
    for part in (up, down, deep):
        rows = part[1024:1040, :].astype(jnp.float32)
        counts = counts + (rows[0:1, :] + rows[1:2, :])

    def total(tile):
        rows = slice(tile * 128, tile * 128 + 128)
        left = own[rows, :] + up[rows, :].astype(jnp.float32)
        right = down[rows, :].astype(jnp.float32) + deep[rows, :].astype(jnp.float32)
        return (left + right).reshape(16, 8, 128)

    for tile in range(0, 8, 2):
        pair = jnp.concatenate([total(tile), total(tile + 1)], axis=1)
        packed[:, tile * 8 : tile * 8 + 16, :] = pair.astype(jnp.bfloat16)
    slab = two_rows(counts)
    for member in range(16):
        packed[member, 64:80, :] = slab


def group_kernel(place, packed, out):
    total = jnp.sum(packed[...].astype(jnp.float32), axis=0)
    for tile in range(8):
        out[tile] = total[tile * 8 : tile * 8 + 8, :]
    lane = lax.broadcasted_iota(jnp.int32, (8, 128), 1)
    wanted = lax.broadcasted_iota(jnp.int32, (8, 128), 0) + place[0] * 8
    counts = jnp.where(lane == wanted, total[64:65, :] + total[65:66, :], 0.0)
    out[8] = jnp.broadcast_to(jnp.sum(counts, axis=1, keepdims=True), (8, 128))


def finish_kernel(core, mine, across, centroids, out):
    part = mine[...] + across[...]
    scale = part[8] + 1.0
    for tile in range(8):
        lanes = slice(tile * 128, tile * 128 + 128)
        held = centroids[:, lanes].astype(jnp.float32)
        held = jnp.where(core[0] == 0, held[:8, :], held[8:, :])
        out[:, lanes] = (part[tile] + held) / scale


def join_kernel(core, mine, other, out):
    first = core[0] == 0
    out[:8, :] = jnp.where(first, mine[...], other[...])
    out[8:, :] = jnp.where(first, other[...], mine[...])


def call(kernel, outs, vmem, operands, scalars=0, scratch=(), flops=0):
    whole = pl.BlockSpec(memory_space=pltpu.VMEM)
    return pl.pallas_call(
        kernel,
        out_shape=[jax.ShapeDtypeStruct(shape, dtype) for shape, dtype in outs],
        in_specs=[pl.BlockSpec(memory_space=pltpu.SMEM)] * scalars + [whole] * (len(operands) - scalars),
        out_specs=[whole] * len(outs),
        scratch_shapes=scratch,
        compiler_params=pltpu.CompilerParams(vmem_limit_bytes=vmem * MIB),
        cost_estimate=pl.CostEstimate(flops=flops, bytes_accessed=MIB, transcendentals=0),
    )(*operands)


def exchange(part):
    return lax.all_to_all(part, BOTH, 0, 0, axis_index_groups=GROUPS, tiled=True)


def body(documents, centroids):
    count, width = documents.shape
    beta = 3.0 / math.sqrt(width)
    blk = lax.axis_index("blk")
    core = lax.axis_index("dp") % 2
    others = lax.ppermute(documents, "dp", within(1))

    near = lax.dynamic_slice_in_dim(centroids, core * 8, 8, 0).reshape(1, 8, width)
    quarter = exchange(jnp.broadcast_to(near, (16, 8, width))).reshape(128, width)
    quarters = [quarter] + [lax.ppermute(quarter, BOTH, star(side, -1)) for side in range(3)]

    flops = 2 * 512 * 2 * count * width
    turned = [
        call(turn_kernel, [((width, count), jnp.bfloat16)], 10, (part,), flops=flops // 64)[0]
        for part in (documents, others)
    ]
    own, up, down, deep = quarters
    logits, stats = [], []
    for held in ((own,), (deep,), (up, down)):
        rows = 128 * len(held)
        part, stat = call(
            functools.partial(logits_kernel, beta, len(stats[-1:])),
            [((rows, 2 * count), jnp.float32), ((4, count), jnp.float32)],
            14,
            (*stats[-1:], *held, *turned),
            scratch=[pltpu.VMEM((rows, width), jnp.bfloat16)],
            flops=flops * rows // 512 // 8,
        )
        logits.append(part)
        stats.append(stat)
    mine = stats[-1]
    theirs = lax.ppermute(mine, "dp", within(1))
    slab = ((1040, 128), jnp.bfloat16)
    normalizer, norms, up, down, deep = call(
        sent_kernel,
        [((1, count), jnp.float32), ((2, count), jnp.float32), slab, slab, slab],
        24,
        (logits[2], logits[1], mine, theirs, documents, others),
        scratch=[pltpu.VMEM((384, 2 * count), jnp.bfloat16)],
        flops=flops,
    )
    (own,) = call(
        own_kernel,
        [((1032, 128), jnp.float32)],
        16,
        (logits[0], norms, documents, others),
        scratch=[pltpu.VMEM((128, 2 * count), jnp.bfloat16)],
        flops=flops // 4,
    )
    sent = (up, down, deep)

    came = [lax.ppermute(part, BOTH, star(side, 1)) for side, part in enumerate(sent)]
    (packed,) = call(star_kernel, [((16, 80, 128), jnp.bfloat16)], 8, (own, *came))
    label = (blk // 16 + 2 * blk) % 4
    place = (blk - jnp.asarray(FIRST)[label]) % 8 * 2 + 1 - blk // 8 % 2
    (part,) = call(
        group_kernel, [((9, 8, 128), jnp.float32)], 4, (place.reshape(1), exchange(packed)), scalars=1
    )
    across = lax.ppermute(part, "dp", within(2))
    (half,) = call(
        finish_kernel,
        [((8, width), jnp.float32)],
        4,
        (core.reshape(1), part, across, centroids),
        scalars=1,
    )
    other = lax.ppermute(half, "dp", within(1))
    (new_centroids,) = call(
        join_kernel, [((16, width), jnp.float32)], 4, (core.reshape(1), half, other), scalars=1
    )
    return (new_centroids, normalizer.reshape(count))


def solution(mesh):
    in_specs = (P(BOTH, None), P("blk", None))
    out_specs = (P("blk", None), P(BOTH))
    return jax.shard_map(body, mesh=mesh, in_specs=in_specs, out_specs=out_specs, check_vma=False)
```

```python
import functools
import math

import jax
import jax.numpy as jnp
from jax import lax
from jax.experimental import pallas as pl
from jax.experimental.pallas import tpu as pltpu
from jax.sharding import PartitionSpec as P

BOTH = ("blk", "dp")
TILE = 512
MIB = 2**20
FIRST = (5, 5, 4, 4)
GROUPS = [
    [
        (((label - 2 * z) % 4 * 2 + x_hi) * 8 + z % 8) * 4 + (x_hi ^ flip) * 2 + core
        for z in range(FIRST[label], FIRST[label] + 8)
        for x_hi in (1, 0)
    ]
    for label in range(4)
    for flip in range(2)
    for core in range(2)
]


def star(side, sign):
    found = []
    for source in range(256):
        blk, dp = divmod(source, 4)
        y, x_hi, z = blk // 16, blk // 8 % 2, blk % 8
        if side == 2:
            z = (z + sign * (1 - 2 * (dp % 2))) % 8
        else:
            y = (y + sign * (1 - 2 * side)) % 4
        found.append((source, ((y * 2 + x_hi) * 8 + z) * 4 + dp))
    return found


def within(bits):
    return [(i, i ^ bits) for i in range(4)]


def turn_kernel(source, out):
    for start in range(0, source.shape[0], TILE):
        out[:, start : start + TILE] = source[start : start + TILE, :].T


def logits_kernel(beta, old, *refs):
    *refs, logits, stats, held = refs
    before, refs = refs[:old], refs[old:]
    *quarters, docs, others = refs
    count = docs.shape[1]
    for i, quarter in enumerate(quarters):
        held[i * 128 : i * 128 + 128, :] = quarter[...]
    block = held[...]
    wide = block.astype(jnp.float32)
    shift = (0.5 * beta) * jnp.sum(wide * wide, axis=1, keepdims=True)
    for side, source in enumerate((docs, others)):
        for start in range(0, count, TILE):
            columns = slice(start, start + TILE)
            part = jnp.dot(block, source[:, columns], preferred_element_type=jnp.float32)
            part = beta * part - shift
            logits[:, side * count + start : side * count + start + TILE] = part
            top = jnp.max(part, axis=0, keepdims=True)
            for stat in before:
                top = jnp.maximum(top, stat[side : side + 1, columns])
            total = jnp.sum(jnp.exp(part - top), axis=0, keepdims=True)
            for stat in before:
                total += stat[2 + side : 3 + side, columns] * jnp.exp(stat[side : side + 1, columns] - top)
            stats[side : side + 1, columns] = top
            stats[2 + side : 3 + side, columns] = total


def two_rows(counts):
    high = counts.astype(jnp.bfloat16)
    rest = (counts - high.astype(jnp.float32)).astype(jnp.bfloat16)
    return jnp.concatenate([high, rest, jnp.zeros((14, 128), jnp.bfloat16)], axis=0)


def write_sums(low, docs, others, counts, outs):
    count = docs.shape[0]
    for i, out in enumerate(outs):
        row = counts[i : i + 1, :]
        if out.dtype == jnp.float32:
            out[1024:1032, :] = jnp.broadcast_to(row, (8, 128))
        else:
            out[1024:1040, :] = two_rows(row)
    for start in range(0, docs.shape[1], 256):
        columns = slice(start, start + 256)
        sums = jnp.dot(low[:, :count], docs[:, columns], preferred_element_type=jnp.float32)
        sums += jnp.dot(low[:, count:], others[:, columns], preferred_element_type=jnp.float32)
        for i, out in enumerate(outs):
            for half in range(2):
                part = sums[i * 128 : i * 128 + 128, half * 128 : half * 128 + 128]
                out[start + half * 128 : start + half * 128 + 128, :] = part.astype(out.dtype)


def weigh(logits, norms, low):
    count = norms.shape[1]
    counts = jnp.zeros((low.shape[0], 128), jnp.float32)
    for side in range(2):
        for start in range(0, count, TILE):
            at = slice(side * count + start, side * count + start + TILE)
            part = jnp.concatenate([ref[:, at] for ref in logits], axis=0)
            weights = jnp.exp(part - norms[side : side + 1, start : start + TILE])
            for k in range(0, TILE, 128):
                counts += weights[:, k : k + 128]
            low[:, at] = weights.astype(jnp.bfloat16)
    flat = jnp.sum(counts.T, axis=0, keepdims=True)
    return jnp.concatenate([flat[:, i : i + 128] for i in range(0, flat.shape[1], 128)], axis=0)


def sent_kernel(pair, deep, mine, theirs, docs, others, normalizer, norms, *refs):
    *outs, low = refs
    for side in range(2):
        a, b = mine[side : side + 1, :], theirs[1 - side : 2 - side, :]
        top = jnp.maximum(a, b)
        total = mine[2 + side : 3 + side, :] * jnp.exp(a - top)
        total += theirs[3 - side : 4 - side, :] * jnp.exp(b - top)
        norms[side : side + 1, :] = top + jnp.log(total)
    normalizer[...] = norms[0:1, :]
    write_sums(low, docs, others, weigh((pair, deep), norms, low), outs)


def own_kernel(own, norms, docs, others, out, low):
    write_sums(low, docs, others, weigh((own,), norms, low), (out,))


def star_kernel(own, up, down, deep, packed):
    counts = own[1024:1025, :]
    for part in (up, down, deep):
        rows = part[1024:1040, :].astype(jnp.float32)
        counts = counts + (rows[0:1, :] + rows[1:2, :])

    def total(tile):
        rows = slice(tile * 128, tile * 128 + 128)
        left = own[rows, :] + up[rows, :].astype(jnp.float32)
        right = down[rows, :].astype(jnp.float32) + deep[rows, :].astype(jnp.float32)
        return (left + right).reshape(16, 8, 128)

    for tile in range(0, 8, 2):
        pair = jnp.concatenate([total(tile), total(tile + 1)], axis=1)
        packed[:, tile * 8 : tile * 8 + 16, :] = pair.astype(jnp.bfloat16)
    slab = two_rows(counts)
    for member in range(16):
        packed[member, 64:80, :] = slab


def group_kernel(place, packed, out):
    total = jnp.sum(packed[...].astype(jnp.float32), axis=0)
    for tile in range(8):
        out[tile] = total[tile * 8 : tile * 8 + 8, :]
    lane = lax.broadcasted_iota(jnp.int32, (8, 128), 1)
    wanted = lax.broadcasted_iota(jnp.int32, (8, 128), 0) + place[0] * 8
    counts = jnp.where(lane == wanted, total[64:65, :] + total[65:66, :], 0.0)
    out[8] = jnp.broadcast_to(jnp.sum(counts, axis=1, keepdims=True), (8, 128))


def finish_kernel(core, mine, across, centroids, out):
    part = mine[...] + across[...]
    scale = part[8] + 1.0
    for tile in range(8):
        lanes = slice(tile * 128, tile * 128 + 128)
        held = centroids[:, lanes].astype(jnp.float32)
        held = jnp.where(core[0] == 0, held[:8, :], held[8:, :])
        out[:, lanes] = (part[tile] + held) / scale


def join_kernel(core, mine, other, out):
    first = core[0] == 0
    out[:8, :] = jnp.where(first, mine[...], other[...])
    out[8:, :] = jnp.where(first, other[...], mine[...])


def call(kernel, outs, vmem, operands, scalars=0, scratch=(), flops=0):
    whole = pl.BlockSpec(memory_space=pltpu.VMEM)
    return pl.pallas_call(
        kernel,
        out_shape=[jax.ShapeDtypeStruct(shape, dtype) for shape, dtype in outs],
        in_specs=[pl.BlockSpec(memory_space=pltpu.SMEM)] * scalars + [whole] * (len(operands) - scalars),
        out_specs=[whole] * len(outs),
        scratch_shapes=scratch,
        compiler_params=pltpu.CompilerParams(vmem_limit_bytes=vmem * MIB),
        cost_estimate=pl.CostEstimate(flops=flops, bytes_accessed=MIB, transcendentals=0),
    )(*operands)


def exchange(part):
    return lax.all_to_all(part, BOTH, 0, 0, axis_index_groups=GROUPS, tiled=True)


def body(documents, centroids):
    count, width = documents.shape
    beta = 3.0 / math.sqrt(width)
    blk = lax.axis_index("blk")
    core = lax.axis_index("dp") % 2

    near = lax.dynamic_slice_in_dim(centroids, core * 8, 8, 0).reshape(1, 8, width)
    quarter = exchange(jnp.broadcast_to(near, (16, 8, width))).reshape(128, width)
    held_docs, quarter = lax.optimization_barrier((documents, quarter))
    others = lax.ppermute(held_docs, "dp", within(1))
    quarters = [quarter] + [lax.ppermute(quarter, BOTH, star(side, -1)) for side in range(3)]

    flops = 2 * 512 * 2 * count * width
    turned = [
        call(turn_kernel, [((width, count), jnp.bfloat16)], 10, (part,), flops=flops // 64)[0]
        for part in (documents, others)
    ]
    own, up, down, deep = quarters
    logits, stats = [], []
    for held in ((own,), (deep,), (up, down)):
        rows = 128 * len(held)
        part, stat = call(
            functools.partial(logits_kernel, beta, len(stats[-1:])),
            [((rows, 2 * count), jnp.float32), ((4, count), jnp.float32)],
            14,
            (*stats[-1:], *held, *turned),
            scratch=[pltpu.VMEM((rows, width), jnp.bfloat16)],
            flops=flops * rows // 512 // 8,
        )
        logits.append(part)
        stats.append(stat)
    mine = stats[-1]
    theirs = lax.ppermute(mine, "dp", within(1))
    slab = ((1040, 128), jnp.bfloat16)
    normalizer, norms, up, down, deep = call(
        sent_kernel,
        [((1, count), jnp.float32), ((2, count), jnp.float32), slab, slab, slab],
        24,
        (logits[2], logits[1], mine, theirs, documents, others),
        scratch=[pltpu.VMEM((384, 2 * count), jnp.bfloat16)],
        flops=flops,
    )
    (own,) = call(
        own_kernel,
        [((1032, 128), jnp.float32)],
        16,
        (logits[0], norms, documents, others),
        scratch=[pltpu.VMEM((128, 2 * count), jnp.bfloat16)],
        flops=flops // 4,
    )
    sent = (up, down, deep)

    came = [lax.ppermute(part, BOTH, star(side, 1)) for side, part in enumerate(sent)]
    (packed,) = call(star_kernel, [((16, 80, 128), jnp.bfloat16)], 8, (own, *came))
    label = (blk // 16 + 2 * blk) % 4
    place = (blk - jnp.asarray(FIRST)[label]) % 8 * 2 + 1 - blk // 8 % 2
    (part,) = call(
        group_kernel, [((9, 8, 128), jnp.float32)], 4, (place.reshape(1), exchange(packed)), scalars=1
    )
    across = lax.ppermute(part, "dp", within(2))
    (half,) = call(
        finish_kernel,
        [((8, width), jnp.float32)],
        4,
        (core.reshape(1), part, across, centroids),
        scalars=1,
    )
    other = lax.ppermute(half, "dp", within(1))
    (new_centroids,) = call(
        join_kernel, [((16, width), jnp.float32)], 4, (core.reshape(1), half, other), scalars=1
    )
    return (new_centroids, normalizer.reshape(count))


def solution(mesh):
    in_specs = (P(BOTH, None), P("blk", None))
    out_specs = (P("blk", None), P(BOTH))
    return jax.shard_map(body, mesh=mesh, in_specs=in_specs, out_specs=out_specs, check_vma=False)
```

```python
import functools
import math

import jax
import jax.numpy as jnp
from jax import lax
from jax.experimental import pallas as pl
from jax.experimental.pallas import tpu as pltpu
from jax.sharding import PartitionSpec as P

BOTH = ("blk", "dp")
TILE = 512
MIB = 2**20
FIRST = (5, 5, 4, 4)
GROUPS = [
    [
        (((label - 2 * z) % 4 * 2 + x_hi) * 8 + z % 8) * 4 + (x_hi ^ flip) * 2 + core
        for z in range(FIRST[label], FIRST[label] + 8)
        for x_hi in (1, 0)
    ]
    for label in range(4)
    for flip in range(2)
    for core in range(2)
]


def star(side, sign):
    found = []
    for source in range(256):
        blk, dp = divmod(source, 4)
        y, x_hi, z = blk // 16, blk // 8 % 2, blk % 8
        if side == 2:
            z = (z + sign * (1 - 2 * (dp % 2))) % 8
        else:
            y = (y + sign * (1 - 2 * side)) % 4
        found.append((source, ((y * 2 + x_hi) * 8 + z) * 4 + dp))
    return found


def within(bits):
    return [(i, i ^ bits) for i in range(4)]


def turn_kernel(source, out):
    for start in range(0, source.shape[0], TILE):
        out[:, start : start + TILE] = source[start : start + TILE, :].T


def logits_kernel(beta, old, *refs):
    *refs, logits, stats, held = refs
    before, refs = refs[:old], refs[old:]
    *quarters, docs, others = refs
    count = docs.shape[1]
    for i, quarter in enumerate(quarters):
        held[i * 128 : i * 128 + 128, :] = quarter[...]
    block = held[...]
    wide = block.astype(jnp.float32)
    shift = (0.5 * beta) * jnp.sum(wide * wide, axis=1, keepdims=True)
    for side, source in enumerate((docs, others)):
        for start in range(0, count, TILE):
            columns = slice(start, start + TILE)
            part = jnp.dot(block, source[:, columns], preferred_element_type=jnp.float32)
            part = beta * part - shift
            logits[:, side * count + start : side * count + start + TILE] = part
            top = jnp.max(part, axis=0, keepdims=True)
            for stat in before:
                top = jnp.maximum(top, stat[side : side + 1, columns])
            total = jnp.sum(jnp.exp(part - top), axis=0, keepdims=True)
            for stat in before:
                total += stat[2 + side : 3 + side, columns] * jnp.exp(stat[side : side + 1, columns] - top)
            stats[side : side + 1, columns] = top
            stats[2 + side : 3 + side, columns] = total


def two_rows(counts):
    high = counts.astype(jnp.bfloat16)
    rest = (counts - high.astype(jnp.float32)).astype(jnp.bfloat16)
    return jnp.concatenate([high, rest, jnp.zeros((14, 128), jnp.bfloat16)], axis=0)


def write_sums(low, docs, others, counts, outs):
    count = docs.shape[0]
    for i, out in enumerate(outs):
        row = counts[i : i + 1, :]
        if out.dtype == jnp.float32:
            out[1024:1032, :] = jnp.broadcast_to(row, (8, 128))
        else:
            out[1024:1040, :] = two_rows(row)
    for start in range(0, docs.shape[1], 256):
        columns = slice(start, start + 256)
        sums = jnp.dot(low[:, :count], docs[:, columns], preferred_element_type=jnp.float32)
        sums += jnp.dot(low[:, count:], others[:, columns], preferred_element_type=jnp.float32)
        for i, out in enumerate(outs):
            for half in range(2):
                part = sums[i * 128 : i * 128 + 128, half * 128 : half * 128 + 128]
                out[start + half * 128 : start + half * 128 + 128, :] = part.astype(out.dtype)


def weigh(logits, norms, low):
    count = norms.shape[1]
    counts = jnp.zeros((low.shape[0], 128), jnp.float32)
    for side in range(2):
        for start in range(0, count, TILE):
            at = slice(side * count + start, side * count + start + TILE)
            part = jnp.concatenate([ref[:, at] for ref in logits], axis=0)
            weights = jnp.exp(part - norms[side : side + 1, start : start + TILE])
            for k in range(0, TILE, 128):
                counts += weights[:, k : k + 128]
            low[:, at] = weights.astype(jnp.bfloat16)
    flat = jnp.sum(counts.T, axis=0, keepdims=True)
    return jnp.concatenate([flat[:, i : i + 128] for i in range(0, flat.shape[1], 128)], axis=0)


def sent_kernel(pair, deep, mine, theirs, docs, others, normalizer, norms, *refs):
    *outs, low = refs
    for side in range(2):
        a, b = mine[side : side + 1, :], theirs[1 - side : 2 - side, :]
        top = jnp.maximum(a, b)
        total = mine[2 + side : 3 + side, :] * jnp.exp(a - top)
        total += theirs[3 - side : 4 - side, :] * jnp.exp(b - top)
        norms[side : side + 1, :] = top + jnp.log(total)
    normalizer[...] = norms[0:1, :]
    write_sums(low, docs, others, weigh((pair, deep), norms, low), outs)


def own_kernel(own, norms, docs, others, out, low):
    write_sums(low, docs, others, weigh((own,), norms, low), (out,))


def star_kernel(own, up, down, deep, packed):
    counts = own[1024:1025, :]
    for part in (up, down, deep):
        rows = part[1024:1040, :].astype(jnp.float32)
        counts = counts + (rows[0:1, :] + rows[1:2, :])

    def total(tile):
        rows = slice(tile * 128, tile * 128 + 128)
        left = own[rows, :] + up[rows, :].astype(jnp.float32)
        right = down[rows, :].astype(jnp.float32) + deep[rows, :].astype(jnp.float32)
        return (left + right).reshape(16, 8, 128)

    for tile in range(0, 8, 2):
        pair = jnp.concatenate([total(tile), total(tile + 1)], axis=1)
        packed[:, tile * 8 : tile * 8 + 16, :] = pair.astype(jnp.bfloat16)
    slab = two_rows(counts)
    for member in range(16):
        packed[member, 64:80, :] = slab


def group_kernel(place, packed, out):
    total = jnp.sum(packed[...].astype(jnp.float32), axis=0)
    for tile in range(8):
        out[tile] = total[tile * 8 : tile * 8 + 8, :]
    lane = lax.broadcasted_iota(jnp.int32, (8, 128), 1)
    wanted = lax.broadcasted_iota(jnp.int32, (8, 128), 0) + place[0] * 8
    counts = jnp.where(lane == wanted, total[64:65, :] + total[65:66, :], 0.0)
    out[8] = jnp.broadcast_to(jnp.sum(counts, axis=1, keepdims=True), (8, 128))


def finish_kernel(core, mine, across, centroids, out):
    part = mine[...] + across[...]
    scale = part[8] + 1.0
    for tile in range(8):
        lanes = slice(tile * 128, tile * 128 + 128)
        held = centroids[:, lanes].astype(jnp.float32)
        held = jnp.where(core[0] == 0, held[:8, :], held[8:, :])
        out[:, lanes] = (part[tile] + held) / scale


def join_kernel(core, mine, other, out):
    first = core[0] == 0
    out[:8, :] = jnp.where(first, mine[...], other[...])
    out[8:, :] = jnp.where(first, other[...], mine[...])


def call(kernel, outs, vmem, operands, scalars=0, scratch=(), flops=0):
    whole = pl.BlockSpec(memory_space=pltpu.VMEM)
    return pl.pallas_call(
        kernel,
        out_shape=[jax.ShapeDtypeStruct(shape, dtype) for shape, dtype in outs],
        in_specs=[pl.BlockSpec(memory_space=pltpu.SMEM)] * scalars + [whole] * (len(operands) - scalars),
        out_specs=[whole] * len(outs),
        scratch_shapes=scratch,
        compiler_params=pltpu.CompilerParams(vmem_limit_bytes=vmem * MIB),
        cost_estimate=pl.CostEstimate(flops=flops, bytes_accessed=MIB, transcendentals=0),
    )(*operands)


def exchange(part):
    return lax.all_to_all(part, BOTH, 0, 0, axis_index_groups=GROUPS, tiled=True)


def body(documents, centroids):
    count, width = documents.shape
    beta = 3.0 / math.sqrt(width)
    blk = lax.axis_index("blk")
    core = lax.axis_index("dp") % 2

    near = lax.dynamic_slice_in_dim(centroids, core * 8, 8, 0).reshape(1, 8, width)
    quarter = exchange(jnp.broadcast_to(near, (16, 8, width))).reshape(128, width)
    held_docs, quarter = lax.optimization_barrier((documents, quarter))
    others = lax.ppermute(held_docs, "dp", within(1))
    quarters = [quarter] + [lax.ppermute(quarter, BOTH, star(side, -1)) for side in range(3)]

    flops = 2 * 512 * 2 * count * width
    turned = [
        call(turn_kernel, [((width, count), jnp.bfloat16)], 10, (part,), flops=flops // 16)[0]
        for part in (documents, others)
    ]
    own, up, down, deep = quarters
    logits, stats = [], []
    for held in ((own,), (deep,), (up, down)):
        rows = 128 * len(held)
        part, stat = call(
            functools.partial(logits_kernel, beta, len(stats[-1:])),
            [((rows, 2 * count), jnp.float32), ((4, count), jnp.float32)],
            14,
            (*stats[-1:], *held, *turned),
            scratch=[pltpu.VMEM((rows, width), jnp.bfloat16)],
            flops=flops * rows // 512 // 8,
        )
        logits.append(part)
        stats.append(stat)
    mine = stats[-1]
    theirs = lax.ppermute(mine, "dp", within(1))
    slab = ((1040, 128), jnp.bfloat16)
    normalizer, norms, up, down, deep = call(
        sent_kernel,
        [((1, count), jnp.float32), ((2, count), jnp.float32), slab, slab, slab],
        24,
        (logits[2], logits[1], mine, theirs, documents, others),
        scratch=[pltpu.VMEM((384, 2 * count), jnp.bfloat16)],
        flops=flops,
    )
    (own,) = call(
        own_kernel,
        [((1032, 128), jnp.float32)],
        16,
        (logits[0], norms, documents, others),
        scratch=[pltpu.VMEM((128, 2 * count), jnp.bfloat16)],
        flops=flops // 4,
    )
    sent = (up, down, deep)

    came = [lax.ppermute(part, BOTH, star(side, 1)) for side, part in enumerate(sent)]
    (packed,) = call(star_kernel, [((16, 80, 128), jnp.bfloat16)], 8, (own, *came))
    label = (blk // 16 + 2 * blk) % 4
    place = (blk - jnp.asarray(FIRST)[label]) % 8 * 2 + 1 - blk // 8 % 2
    (part,) = call(
        group_kernel, [((9, 8, 128), jnp.float32)], 4, (place.reshape(1), exchange(packed)), scalars=1
    )
    across = lax.ppermute(part, "dp", within(2))
    (half,) = call(
        finish_kernel,
        [((8, width), jnp.float32)],
        4,
        (core.reshape(1), part, across, centroids),
        scalars=1,
    )
    other = lax.ppermute(half, "dp", within(1))
    (new_centroids,) = call(
        join_kernel, [((16, width), jnp.float32)], 4, (core.reshape(1), half, other), scalars=1
    )
    return (new_centroids, normalizer.reshape(count))


def solution(mesh):
    in_specs = (P(BOTH, None), P("blk", None))
    out_specs = (P("blk", None), P(BOTH))
    return jax.shard_map(body, mesh=mesh, in_specs=in_specs, out_specs=out_specs, check_vma=False)
```
